128 devices in a mesh: section: 8 (over y, x_hi), dp: 4 (over x_lo, core), tensor: 4 (over z).
Axes of the slice: x: 4 (x_hi: 2, x_lo: 2; x = x_hi * 2 + x_lo), y: 4, z: 4, core: 2. Of those that a mesh axis runs over, the one named last changes fastest.
Arguments:
- earlier_inputs: bfloat16 [8, 2048, 12288], P('section', 'dp'), may hold values from -6 to 6
- earlier_grads: bfloat16 [8, 2048, 2048], P('section', 'dp', 'tensor'), may hold values from -6 to 6
- current_grads: bfloat16 [8, 2048, 2048], P('section', 'dp', 'tensor'), may hold values from -6 to 6
- key_value_weight: bfloat16 [8, 12288, 2048], P('section', 'dp', 'tensor'), may hold values from -0.078125 to 0.078125
- exponents: int32 [8, 96, 2048], P('section', 'tensor', 'dp'), may hold values from -11 to -9
- sign_bits: int32 [12288], P('tensor'), may hold values from 0 to 1
Outputs:
- upstream_grad: bfloat16 [8, 12288, 2048], P('section', 'tensor', 'dp')
- weight_grad: float32 [8, 12288, 2048], P('section', 'dp', 'tensor')
The draws below stay inside these ranges and needn't reach their ends.
Inputs may be any that keep to these rules, and one draw needn't show every extreme that they name: exponents of the power-of-two scales.
All inputs are finite; a program needn't handle non-finite values.
Results may differ from the reference program's by a relative error of at most 0.0038.
Values may be sent and summed in bfloat16 or wider, within the bound.
No kernel may reach another device: no remote copies, remote signals or barrier semaphores. Data moves between devices by JAX's collectives and lax.ppermute only.
A program may use at most 192 MiB of HBM per device.

```python
import jax
import jax.numpy as jnp
from jax import lax

D = 12288
HB = 128
SECTIONS = 8
TOKENS = 2048
KVW = 2048


def place_ends(drawn, stream_key, smallest, high):
    index_at = [jax.random.randint(jax.random.fold_in(stream_key, axis), (), 0, length) for axis, length in enumerate(drawn.shape)]
    longest = drawn.shape.index(max(drawn.shape))
    next_to = index_at[:longest] + [(index_at[longest] + 1) % drawn.shape[longest]] + index_at[longest + 1:]
    return drawn.at[tuple(index_at)].set(smallest).at[tuple(next_to)].set(high)


def spiked(entries, rng, source, target, blocks, factor):
    def block_of(position):
        return (jnp.arange(entries.shape[position]) // (entries.shape[position] // blocks)).reshape((-1,) + (1,) * (entries.ndim - 1 - position))

    one_side = jax.random.permutation(rng, blocks)[block_of(target)]
    far = (block_of(target) + blocks // 2) % blocks
    return jnp.where((block_of(source) == one_side) | (block_of(source) == far), factor * entries, entries)


def block_levels(stream_key, shape, cuts, least, top_value):
    loudness, own = 1.0, jax.random.fold_in(stream_key, 6)
    for position, blocks in cuts:
        draws = jnp.exp(jax.random.uniform(jax.random.fold_in(own, position), (blocks,), jnp.float32, least / len(cuts), top_value / len(cuts)))
        loudness = loudness * jnp.repeat(draws, shape[position] // blocks).reshape([-1 if axis == position else 1 for axis in range(len(shape))])
    return loudness


def bell_draw(rng, shape, deviation, reach, shards=(), held_as=jnp.bfloat16):
    result = deviation * jax.random.normal(rng, shape, jnp.float32)
    if shards:
        result = result * block_levels(rng, shape, shards, -0.22, 0.18)
    return jnp.clip(result, -reach, reach).astype(held_as)


def noise_with(stream_key, dims, spread, bound, pieces, heavy, kind=jnp.bfloat16):
    result = spread * jax.random.normal(stream_key, dims, jnp.float32)
    if pieces:
        result = result * block_levels(stream_key, dims, pieces, -0.22, 0.18)
    return jnp.clip(spiked(result, jax.random.fold_in(stream_key, 3), *heavy), -bound, bound).astype(kind)


def setup_inputs(seed: int = 0) -> dict:
    arg_keys = jax.random.split(jax.random.key(seed), 7)
    earlier_inputs = noise_with(arg_keys[0], (SECTIONS, TOKENS, D), 1.0, 6.0, ((0, 8), (1, 4)), (1, 2, 4, 2.0))
    earlier_grads = bell_draw(arg_keys[1], (SECTIONS, TOKENS, KVW), 1.0, 6.0, ((0, 8), (1, 4), (2, 4)))
    current_grads = bell_draw(arg_keys[2], (SECTIONS, TOKENS, KVW), 1.0, 6.0, ((0, 8), (1, 4), (2, 4)))
    key_value_weight = noise_with(arg_keys[3], (SECTIONS, D, KVW), D ** -0.5, 0.078125, ((0, 8), (1, 4), (2, 4)), (2, 1, 4, 2.0))
    exponents = place_ends(jax.random.randint(arg_keys[4], (SECTIONS, D // HB, TOKENS), -11, -8), jax.random.fold_in(arg_keys[4], 1), -11, (-8) - 1).astype(jnp.int32)
    sign_bits = place_ends(jax.random.randint(arg_keys[5], (D,), 0, 2), jax.random.fold_in(arg_keys[5], 1), 0, 1).astype(jnp.int32)
    return dict(earlier_inputs=earlier_inputs, earlier_grads=earlier_grads, current_grads=current_grads, key_value_weight=key_value_weight, exponents=exponents, sign_bits=sign_bits)


fp8_limit = 448.0

def hadamard_table():
    index = jnp.arange(HB, dtype=jnp.int32)
    table = jnp.ones((HB, HB), jnp.float32)
    for bit_pos in range(HB.bit_length() - 1):
        both = (index[:, None] >> bit_pos & 1) * (index[None, :] >> bit_pos & 1)
        table = table * (1.0 - 2.0 * both.astype(jnp.float32))
    return table / jnp.sqrt(jnp.float32(HB))

def reference(earlier_inputs, earlier_grads, current_grads, key_value_weight, exponents, sign_bits):
    table = hadamard_table()
    signs = (2 * sign_bits - 1).astype(jnp.float32)
    weight_list = []
    coded_list = []
    for section_id in range(SECTIONS):
        weight_list.append(lax.dot_general(earlier_inputs[section_id], earlier_grads[section_id], (((0,), (0,)), ((), ())), preferred_element_type=jnp.float32))
        input_grad = lax.dot_general(key_value_weight[section_id], current_grads[section_id], (((1,), (1,)), ((), ())), preferred_element_type=jnp.float32)
        blocks = (input_grad * signs[:, None]).reshape(D // HB, HB, TOKENS)
        rotated = jnp.einsum('ij,bjt->bit', table, blocks, precision=lax.Precision.HIGHEST)
        scale = jnp.exp2(-exponents[section_id].astype(jnp.float32))
        coded_list.append(jnp.clip(rotated * scale[:, None, :], -fp8_limit, fp8_limit).astype(jnp.bfloat16))
    outputs = []
    for section_id in range(SECTIONS):
        if section_id + 1 < SECTIONS:
            values = coded_list[section_id + 1].astype(jnp.float32) * jnp.exp2(exponents[section_id + 1].astype(jnp.float32))[:, None, :]
            back = jnp.einsum('ji,bjt->bit', table, values, precision=lax.Precision.HIGHEST).reshape(D, TOKENS)
            outputs.append((back * signs[:, None]).astype(jnp.bfloat16))
        else:
            outputs.append(jnp.zeros((D, TOKENS), jnp.bfloat16))
    return (jnp.stack(outputs), jnp.stack(weight_list))
```

```python
import jax
import jax.numpy as jnp
from jax import lax
from jax.experimental import pallas as pl
from jax.experimental.pallas import tpu as pltpu
from jax.sharding import PartitionSpec as P

HB = 128
FP8_LIMIT = 448.0
AXES = ("section", "dp", "tensor")
VMEM = pl.BlockSpec(memory_space=pltpu.VMEM)
SMEM = pl.BlockSpec(memory_space=pltpu.SMEM)


def send(shard, place):
    sections, dps, tensors = (lax.axis_size(axis) for axis in AXES)
    pairs = []
    for s in range(sections):
        for d in range(dps):
            for t in range(tensors):
                to_s, to_d, to_t = place(s, d, t)
                if 0 <= to_s < sections:
                    pairs.append(((s * dps + d) * tensors + t, (to_s * dps + to_d) * tensors + to_t % tensors))
    return lax.ppermute(shard, AXES, pairs)


def other_core(shard):
    return send(shard, lambda s, d, t: (s, d ^ 1, t))


def other_chip(shard):
    return send(shard, lambda s, d, t: (s, d ^ 2, t))


def hadamard_signs(order):
    index = jnp.arange(order, dtype=jnp.int32)
    table = jnp.ones((order, order), jnp.float32)
    for bit_pos in range(order.bit_length() - 1):
        both = (index[:, None] >> bit_pos & 1) * (index[None, :] >> bit_pos & 1)
        table = table * (1.0 - 2.0 * both.astype(jnp.float32))
    return table


def rotate_kernel(base_ref, w0, w1, w2, w3, table_ref, g0, g1, g2, g3, out_ref):
    base = base_ref[0]
    weights, grads = (w0, w1, w2, w3), (g0, g1, g2, g3)
    rows, depth = w0.shape
    norm = HB ** -0.5
    for k, grad in enumerate(grads):
        slot = jnp.bitwise_xor(base, k)

        @pl.loop(0, rows // (2 * HB))
        def _(m):
            at = pl.multiple_of(m * 2 * HB, 2 * HB)
            total = None
            for r, weight in enumerate(weights):
                term = lax.dot_general(
                    weight[pl.ds(at, 2 * HB), :],
                    grad[:, r * depth : (r + 1) * depth],
                    (((1,), (1,)), ((), ())),
                    preferred_element_type=jnp.float32,
                )
                total = term if total is None else total + term
            high = total.astype(jnp.bfloat16)
            low = (total - high.astype(jnp.float32)).astype(jnp.bfloat16)
            for b in range(2):
                both = jnp.concatenate([high[b * HB : (b + 1) * HB], low[b * HB : (b + 1) * HB]], axis=0)
                turned = jnp.dot(table_ref[m * 2 + b], both, preferred_element_type=jnp.float32) * norm
                out_ref[slot, pl.ds(pl.multiple_of(at + b * HB, HB), HB), :] = turned.astype(jnp.bfloat16)


def rotate(base, weights, table, grads):
    rows, depth = weights[0].shape
    tokens = grads[0].shape[0]
    flops = 2 * rows * len(grads) * tokens * depth * len(weights)
    return pl.pallas_call(
        rotate_kernel,
        out_shape=jax.ShapeDtypeStruct((len(grads), rows, tokens), jnp.bfloat16),
        in_specs=[SMEM] + [VMEM] * 9,
        out_specs=VMEM,
        compiler_params=pltpu.CompilerParams(vmem_limit_bytes=40 * 1024 * 1024),
        cost_estimate=pl.CostEstimate(flops=flops, bytes_accessed=16 << 20, transcendentals=0),
        name="rotate",
    )(base, *weights, table, *grads)


def back_kernel(here_ref, p0, p1, p2, p3, limit_ref, table_ref, out_ref):
    here = here_ref[0]
    pieces = (p0, p1, p2, p3)
    blocks = p0.shape[0] // HB
    norm = HB ** -0.5
    for r, piece in enumerate(pieces):
        first = jnp.bitwise_xor(here, r) * blocks

        @pl.loop(0, blocks)
        def _(b):
            limit = limit_ref[first + b]
            values = piece[pl.ds(pl.multiple_of(b * HB, HB), HB), :].astype(jnp.float32)
            values = jnp.clip(values, -limit, limit).astype(jnp.bfloat16)
            turned = jnp.dot(table_ref[first + b], values, preferred_element_type=jnp.float32) * norm
            out_ref[pl.ds(pl.multiple_of((first + b) * HB, HB), HB), :] = turned.astype(jnp.bfloat16)


def back(here, pieces, limit, table):
    rows, tokens = pieces[0].shape
    return pl.pallas_call(
        back_kernel,
        out_shape=jax.ShapeDtypeStruct((len(pieces) * rows, tokens), jnp.bfloat16),
        in_specs=[SMEM] + [VMEM] * 6,
        out_specs=VMEM,
        compiler_params=pltpu.CompilerParams(vmem_limit_bytes=40 * 1024 * 1024),
        cost_estimate=pl.CostEstimate(flops=2 * 4 * rows * tokens * HB, bytes_accessed=7 << 20, transcendentals=0),
        name="rotate_back",
    )(here, *pieces, limit, table)


def body(earlier_inputs, earlier_grads, current_grads, key_value_weight, exponents, sign_bits):
    dp, tensor = lax.axis_index("dp"), lax.axis_index("tensor")
    parts = lax.axis_size("tensor")
    inputs_local, grads_before = earlier_inputs[0], earlier_grads[0]
    rows_here = key_value_weight.shape[1]
    quarter = rows_here // parts

    def scalar(value):
        return jnp.reshape(value, (1,)).astype(jnp.int32)

    grads_far = send(current_grads[0], lambda s, d, t: (s - 1, d ^ 2, t))
    grads_near = other_chip(grads_far)
    pieces_of = []
    for held in (grads_near, grads_far):
        around = [held] + [send(held, lambda s, d, t, r=r: (s, d, t + r)) for r in range(1, parts)]
        pieces_of.append(jnp.concatenate(around, axis=1))
    near, far = pieces_of
    grads = [near, other_core(near), far, other_core(far)]
    weights = []
    for r in range(parts):
        piece = lax.dynamic_slice_in_dim(key_value_weight[0], (tensor + r) % parts * quarter, quarter, 0)
        weights.append(send(piece, lambda s, d, t, r=r: (s - 1, d ^ 2, t + r)))

    plain = hadamard_signs(HB)
    bits = lax.dynamic_slice_in_dim(sign_bits, dp * quarter, quarter, 0)
    bits = send(bits, lambda s, d, t: (s, t ^ 2, d))
    signs_there = (2 * bits - 1).astype(jnp.float32).reshape(-1, 1, HB)
    table = (plain * signs_there).astype(jnp.bfloat16)
    turned = rotate(
        scalar(jnp.bitwise_xor(dp, tensor)), weights, jnp.concatenate([table, table], axis=2), grads
    )
    pieces = [send(turned[r], lambda s, d, t, r=r: (s, t ^ r, d ^ 2)) for r in range(parts)]
    got_expo = send(exponents[0], lambda s, d, t: (s - 1, d, t))
    limit = (FP8_LIMIT * jnp.exp2(got_expo.astype(jnp.float32)))[:, None, :]
    signs_here = (2 * sign_bits - 1).astype(jnp.float32).reshape(-1, HB, 1)
    upstream_grad = back(scalar(dp), pieces, limit, (plain * signs_here).astype(jnp.bfloat16))

    def features(block):
        return lax.dynamic_slice_in_dim(inputs_local, block * rows_here, rows_here, 1)

    def product(mine, got):
        return lax.dot_general(
            mine, grads_before, (((0,), (0,)), ((), ())), preferred_element_type=jnp.float32
        ) + lax.dot_general(got, grads_other, (((0,), (0,)), ((), ())), preferred_element_type=jnp.float32)

    grads_other = other_core(grads_before)
    got_far = other_core(features(jnp.bitwise_xor(dp, 3)))
    got_near = other_core(features(jnp.bitwise_xor(dp, 1)))
    partial = product(features(jnp.bitwise_xor(dp, 2)), got_far).astype(jnp.bfloat16)
    arrived = other_chip(partial).astype(jnp.float32)
    weight_grad = product(features(dp), got_near) + arrived
    return (upstream_grad[None], weight_grad[None])


def solution(mesh):
    placed = (
        P("section", "dp", None),
        P("section", "dp", "tensor"),
        P("section", "dp", "tensor"),
        P("section", "dp", "tensor"),
        P("section", "tensor", "dp"),
        P("tensor"),
    )
    return jax.shard_map(
        body,
        mesh=mesh,
        in_specs=placed,
        out_specs=(P("section", "tensor", "dp"), P("section", "dp", "tensor")),
        check_vma=False,
    )
```

```python
import functools

import jax
import jax.numpy as jnp
from jax import lax
from jax.experimental import pallas as pl
from jax.experimental.pallas import tpu as pltpu
from jax.sharding import Mesh
from jax.sharding import PartitionSpec as P

HB = 128
FP8_LIMIT = 448.0
LONG = 100_000_000_000
AXES = ("section", "chip", "core", "tensor")
VMEM = pl.BlockSpec(memory_space=pltpu.VMEM)
SMEM = pl.BlockSpec(memory_space=pltpu.SMEM)


def send(shard, place):
    sections, chips, cores, tensors = (lax.axis_size(axis) for axis in AXES)
    dps = chips * cores
    pairs = []
    for s in range(sections):
        for d in range(dps):
            for t in range(tensors):
                to_s, to_d, to_t = place(s, d, t)
                if 0 <= to_s < sections:
                    pairs.append(((s * dps + d) * tensors + t, (to_s * dps + to_d) * tensors + to_t % tensors))
    return lax.ppermute(shard, AXES, pairs)


def other_core(shard):
    return send(shard, lambda s, d, t: (s, d ^ 1, t))


def other_chip(shard):
    return send(shard, lambda s, d, t: (s, d ^ 2, t))


def signs_kernel(table_ref):
    order = table_ref.shape[0]
    both = lax.broadcasted_iota(jnp.int32, (order, order), 0) & lax.broadcasted_iota(jnp.int32, (order, order), 1)
    odd = jnp.zeros_like(both)
    for bit in range(order.bit_length() - 1):
        odd = odd ^ (both >> bit & 1)
    table_ref[...] = (1 - 2 * odd).astype(jnp.float32)


def hadamard_signs(order):
    return pl.pallas_call(
        signs_kernel,
        out_shape=jax.ShapeDtypeStruct((order, order), jnp.float32),
        out_specs=VMEM,
        cost_estimate=pl.CostEstimate(flops=LONG, bytes_accessed=0, transcendentals=0),
        name="hadamard_signs",
    )()


def sign_table_kernel(plain_ref, signs_ref, out_ref):
    for b in range(out_ref.shape[0]):
        out_ref[b] = (plain_ref[...] * signs_ref[b]).astype(jnp.bfloat16)


def sign_table(plain, bits):
    signs = (2 * bits - 1).astype(jnp.float32).reshape(-1, HB, 1)
    return pl.pallas_call(
        sign_table_kernel,
        out_shape=jax.ShapeDtypeStruct((signs.shape[0], HB, HB), jnp.bfloat16),
        in_specs=[VMEM] * 2,
        out_specs=VMEM,
        cost_estimate=pl.CostEstimate(flops=0, bytes_accessed=0, transcendentals=0),
        name="sign_table",
    )(plain, signs)


def after(value, *others):
    return lax.optimization_barrier((value, *others))[0]


def rotate_kernel(place_ref, *refs):
    base, core = place_ref[0], place_ref[1]
    own, other, (table_ref, held_ref, a_ref, b_ref), outs = refs[:2], refs[2:4], refs[4:8], refs[8:]
    rows = own[0].shape[0] // 2
    tokens = outs[0].shape[1]
    norm = HB ** -0.5
    for k in range(4):
        slot = jnp.bitwise_xor(base, k)
        weights = own if k % 2 == 0 else other
        near = k // 2 * tokens
        total = None
        for x in range(4):
            at = slice(near, near + tokens)
            turn = core if x == 1 else 1 - core
            place = pl.ds(pl.multiple_of(turn * rows, rows), rows) if x % 2 else slice(x // 2 * rows, (x // 2 + 1) * rows)
            weight = weights[(x + 1) % 2][place, :]
            grads = (held_ref[at, :], a_ref[at, :], b_ref[1, at, :], b_ref[0, at, :])[x]
            term = lax.dot_general(weight, grads, (((1,), (1,)), ((), ())), preferred_element_type=jnp.float32)
            total = term if total is None else total + term
        high = total.astype(jnp.bfloat16)
        low = (total - high.astype(jnp.float32)).astype(jnp.bfloat16)
        turned = []
        for b in range(rows // HB):
            rows_at = slice(b * HB, (b + 1) * HB)
            both = jnp.concatenate([high[rows_at], low[rows_at]], axis=0)
            table = table_ref[k % 2 * (rows // HB) + b]
            turned.append((jnp.dot(table, both, preferred_element_type=jnp.float32) * norm).astype(jnp.bfloat16))
        done = jnp.concatenate(turned, axis=0)
        for r, out_ref in enumerate(outs):

            @pl.when(slot == r)
            def _():
                out_ref[...] = done


def rotate(place, weights, table, grads):
    rows = weights[0].shape[0] // 2
    tokens = grads[0].shape[0] // 2
    return pl.pallas_call(
        rotate_kernel,
        out_shape=[jax.ShapeDtypeStruct((rows, tokens), jnp.bfloat16)] * 4,
        in_specs=[SMEM] + [VMEM] * 8,
        out_specs=[VMEM] * 4,
        compiler_params=pltpu.CompilerParams(vmem_limit_bytes=40 * 1024 * 1024),
        cost_estimate=pl.CostEstimate(flops=0, bytes_accessed=0, transcendentals=0),
        name="rotate",
    )(place, *weights, table, *grads)


def back_kernel(here_ref, p0, p1, p2, p3, limit_ref, table_ref, out_ref):
    here = here_ref[0]
    pieces = (p0, p1, p2, p3)
    blocks = p0.shape[0] // HB
    norm = HB ** -0.5
    for r, piece in enumerate(pieces):
        first = jnp.bitwise_xor(here, r) * blocks

        for b in range(blocks):
            limit = limit_ref[first + b]
            values = piece[b * HB : (b + 1) * HB, :].astype(jnp.float32)
            values = jnp.clip(values, -limit, limit).astype(jnp.bfloat16)
            turned = jnp.dot(table_ref[first + b], values, preferred_element_type=jnp.float32) * norm
            out_ref[pl.ds(pl.multiple_of((first + b) * HB, HB), HB), :] = turned.astype(jnp.bfloat16)


def back(here, pieces, limit, table):
    rows, tokens = pieces[0].shape
    return pl.pallas_call(
        back_kernel,
        out_shape=jax.ShapeDtypeStruct((len(pieces) * rows, tokens), jnp.bfloat16),
        in_specs=[SMEM] + [VMEM] * 6,
        out_specs=VMEM,
        compiler_params=pltpu.CompilerParams(vmem_limit_bytes=40 * 1024 * 1024),
        cost_estimate=pl.CostEstimate(flops=2 * 4 * rows * tokens * HB, bytes_accessed=7 << 20, transcendentals=0),
        name="rotate_back",
    )(here, *pieces, limit, table)


def product_kernel(skip, arrived, block_ref, inputs_ref, got_ref, grads_ref, other_ref, *rest):
    arrived, outs, (held, done) = rest[:arrived], rest[arrived:-2], rest[-2:]
    tile = held.shape[2]
    tiles = (got_ref.shape[1] - skip) // tile
    sum_rows = (((0,), (0,)), ((), ()))
    start = block_ref[0] * tiles

    def fetch(i):
        at = pl.ds(pl.multiple_of((start + i) * tile, tile), tile)
        return pltpu.make_async_copy(inputs_ref.at[:, at], held.at[i % 2], done.at[i % 2])

    fetch(0).start()
    for i in range(tiles):
        if i + 1 < tiles:
            fetch(i + 1).start()
        fetch(i).wait()
        got = got_ref[:, skip + i * tile : skip + (i + 1) * tile]
        total = lax.dot_general(held[i % 2], grads_ref[...], sum_rows, preferred_element_type=jnp.float32)
        other = other_ref[:, : grads_ref.shape[1]]
        total += lax.dot_general(got, other, sum_rows, preferred_element_type=jnp.float32)

        def part(refs):
            row = i * tile
            for ref in refs:
                if row < ref.shape[0]:
                    return ref.at[row : row + tile, :]
                row -= ref.shape[0]

        if arrived:
            total += part(arrived)[...].astype(jnp.float32)
        part(outs)[...] = total.astype(outs[0].dtype)


def product(inputs, block, got, grads, other, dtype, outs, skip=0, arrived=()):
    tokens, columns = grads.shape
    rows = got.shape[1] - skip
    return pl.pallas_call(
        functools.partial(product_kernel, skip, len(arrived)),
        out_shape=[jax.ShapeDtypeStruct((rows // 4 * quarters, columns), dtype) for quarters in outs],
        in_specs=[SMEM, pl.BlockSpec(memory_space=pltpu.HBM)] + [VMEM] * (3 + len(arrived)),
        out_specs=[VMEM] * len(outs),
        scratch_shapes=[pltpu.VMEM((2, tokens, rows // 4), inputs.dtype), pltpu.SemaphoreType.DMA((2,))],
        compiler_params=pltpu.CompilerParams(vmem_limit_bytes=40 * 1024 * 1024),
        cost_estimate=pl.CostEstimate(flops=0, bytes_accessed=0, transcendentals=0),
        name="weight_product",
    )(block, inputs, got, grads, other, *arrived)


def body(earlier_inputs, earlier_grads, current_grads, key_value_weight, exponents, sign_bits):
    chip, core, tensor = (lax.axis_index(axis) for axis in AXES[1:])
    dp = chip * lax.axis_size("core") + core
    parts = lax.axis_size("tensor")
    inputs_local, grads_before, weight_local = earlier_inputs[0], earlier_grads[0], key_value_weight[0]
    rows_here = weight_local.shape[0]
    quarter = rows_here // parts

    def scalar(value):
        return jnp.reshape(value, (1,)).astype(jnp.int32)

    def features(inputs, block):
        return lax.dynamic_slice_in_dim(inputs, block * rows_here, rows_here, 1)

    def down(shard, turn=0):
        return send(shard, lambda s, d, t: (s - 1, d ^ 2, t ^ turn))

    def over_z(shard, x):
        return send(shard, lambda s, d, t: (s, d, t ^ x))

    quarters = [
        lax.dynamic_slice_in_dim(weight_local, jnp.bitwise_xor(tensor, x) * quarter, quarter, 0) for x in range(parts)
    ]

    tokens, columns = current_grads.shape[1:]
    plain = hadamard_signs(HB)
    dealt = [quarters[0], over_z(quarters[1], 1), None, over_z(quarters[3], 3)]
    limit = (FP8_LIMIT * jnp.exp2(exponents[0].astype(jnp.float32))).astype(jnp.bfloat16)
    blocks = limit.shape[0]
    limit = jnp.pad(limit, ((0, -blocks % 16), (0, 0)))
    grads_far = down(jnp.concatenate([current_grads[0], limit], axis=0))

    inputs_then = after(inputs_local, quarters[1])
    got_far = other_core(jnp.concatenate([grads_before, features(inputs_then, jnp.bitwise_xor(dp, 3))], axis=1))
    (partial,) = product(
        inputs_local, scalar(jnp.bitwise_xor(dp, 2)), got_far, grads_before, got_far, jnp.bfloat16, (4,), columns
    )
    grads_far, dealt[1], dealt[3], partial, second = lax.optimization_barrier(
        (grads_far, dealt[1], dealt[3], partial, quarters[2])
    )

    dealt[2] = over_z(second, 2)
    grads_near = other_chip(grads_far)
    half = down(jnp.concatenate([dealt[1], dealt[3]], axis=0))
    arrived = other_chip(after(partial, grads_near))
    bits = lax.dynamic_slice_in_dim(sign_bits, dp * quarter, quarter, 0)
    bits = send(bits, lambda s, d, t: (s, t ^ 2, d))
    other_half = down(after(jnp.concatenate([dealt[0], dealt[2]], axis=0), grads_near))
    got_near = other_core(features(after(inputs_local, grads_near), jnp.bitwise_xor(dp, 1)))
    here = sign_table(plain, sign_bits)
    grads_near, plain, bits, here = lax.optimization_barrier((grads_near, plain, bits, here))

    limit = grads_near[tokens : tokens + blocks]
    held = jnp.concatenate([grads_near[:tokens], grads_far[:tokens]], axis=0)
    step_a = send(held, lambda s, d, t: (s, d, t ^ (3 if d & 1 else 1)))
    step_a, half, bits_other = lax.optimization_barrier((step_a, half, other_core(bits)))
    step_b = send(jnp.stack([held, step_a]), lambda s, d, t: (s, d, t ^ (1 if d & 1 else 3)))
    weights = (half, other_half, other_core(half), other_core(other_half))
    bits = jnp.concatenate([bits, bits_other])
    step_b, got_near, *weights = lax.optimization_barrier((step_b, got_near, *weights))

    signs_there = (2 * bits - 1).astype(jnp.float32).reshape(-1, 1, HB)
    table = (plain * signs_there).astype(jnp.bfloat16)
    turned = rotate(
        jnp.stack([jnp.bitwise_xor(dp, tensor), core]).astype(jnp.int32),
        weights,
        jnp.concatenate([table, table], axis=2),
        (held, step_a, step_b),
    )

    arrived, *later = lax.optimization_barrier((arrived, *turned[2:]))
    turned = [*turned[:2], *later]

    pieces = [
        send(turned[r], lambda s, d, t, r=r: (s, (t ^ r) & 2 | d & 1, (d & 2 ^ 2) | (t ^ r) & 1)) for r in range(parts)
    ]
    limit = limit.astype(jnp.float32)[:, None, :]
    (weight_grad,) = product(
        inputs_local, scalar(dp), got_near, grads_before, got_far, jnp.float32, (4,), 0, (arrived,)
    )
    place = scalar(chip * 2 + jnp.bitwise_and(tensor, 1))
    upstream_grad = back(place, pieces, limit, here)
    return (upstream_grad[None], weight_grad[None])


def solution(mesh):
    sections, dps, tensors = (mesh.shape[axis] for axis in ("section", "dp", "tensor"))
    split = Mesh(mesh.devices.reshape(sections, dps // 2, 2, tensors), AXES)
    dp = ("chip", "core")
    placed = (
        P("section", dp, None),
        P("section", dp, "tensor"),
        P("section", dp, "tensor"),
        P("section", dp, "tensor"),
        P("section", "tensor", dp),
        P("tensor"),
    )
    return jax.shard_map(
        body,
        mesh=split,
        in_specs=placed,
        out_specs=(P("section", "tensor", dp), P("section", dp, "tensor")),
        check_vma=False,
    )
```

```python
import functools

import jax
import jax.numpy as jnp
from jax import lax
from jax.experimental import pallas as pl
from jax.experimental.pallas import tpu as pltpu
from jax.sharding import Mesh
from jax.sharding import PartitionSpec as P

HB = 128
FP8_LIMIT = 448.0
LONG = 100_000_000_000
AXES = ("section", "chip", "core", "tensor")
VMEM = pl.BlockSpec(memory_space=pltpu.VMEM)
SMEM = pl.BlockSpec(memory_space=pltpu.SMEM)


def send(shard, place):
    sections, chips, cores, tensors = (lax.axis_size(axis) for axis in AXES)
    dps = chips * cores
    pairs = []
    for s in range(sections):
        for d in range(dps):
            for t in range(tensors):
                to_s, to_d, to_t = place(s, d, t)
                if 0 <= to_s < sections:
                    pairs.append(((s * dps + d) * tensors + t, (to_s * dps + to_d) * tensors + to_t % tensors))
    return lax.ppermute(shard, AXES, pairs)


def other_core(shard):
    return send(shard, lambda s, d, t: (s, d ^ 1, t))


def other_chip(shard):
    return send(shard, lambda s, d, t: (s, d ^ 2, t))


def signs_kernel(table_ref):
    order = table_ref.shape[0]
    both = lax.broadcasted_iota(jnp.int32, (order, order), 0) & lax.broadcasted_iota(jnp.int32, (order, order), 1)
    odd = jnp.zeros_like(both)
    for bit in range(order.bit_length() - 1):
        odd = odd ^ (both >> bit & 1)
    table_ref[...] = (1 - 2 * odd).astype(jnp.float32)


def hadamard_signs(order):
    return pl.pallas_call(
        signs_kernel,
        out_shape=jax.ShapeDtypeStruct((order, order), jnp.float32),
        out_specs=VMEM,
        cost_estimate=pl.CostEstimate(flops=LONG, bytes_accessed=0, transcendentals=0),
        name="hadamard_signs",
    )()


def after(value, *others):
    return lax.optimization_barrier((value, *others))[0]


def rotated_rows(pair, rest, table_ref, grads_refs, swapped, far):
    held_ref, a_ref, b_ref = grads_refs
    rows, tokens = pair.shape[0] // 2, held_ref.shape[0] // 2
    at = slice(far * tokens, (far + 1) * tokens)
    first, second = slice(0, rows), slice(rows, 2 * rows)
    total = None
    for weight, grads in (
        (rest[first, :], held_ref[at, :]),
        (pair[second if swapped else first, :], a_ref[at, :]),
        (pair[first if swapped else second, :], b_ref[0, at, :]),
        (rest[second, :], b_ref[1, at, :]),
    ):
        term = lax.dot_general(weight, grads, (((1,), (1,)), ((), ())), preferred_element_type=jnp.float32)
        total = term if total is None else total + term
    high = total.astype(jnp.bfloat16)
    low = (total - high.astype(jnp.float32)).astype(jnp.bfloat16)
    turned = []
    for b in range(rows // HB):
        both = jnp.concatenate([high[b * HB : (b + 1) * HB], low[b * HB : (b + 1) * HB]], axis=0)
        turned.append((jnp.dot(table_ref[b], both, preferred_element_type=jnp.float32) * HB**-0.5).astype(jnp.bfloat16))
    return jnp.concatenate(turned, axis=0)


def rotate_kernel(base_ref, table_ref, *refs):
    base = base_ref[0]
    given, outs, inside, made, come, gone = refs[:7], refs[7:11], refs[11:18], refs[18], refs[19], refs[20]
    fetches = [pltpu.make_async_copy(far, near, come.at[i]) for i, (far, near) in enumerate(zip(given, inside))]
    for fetch in fetches:
        fetch.start()
    grads, weights = inside[:3], inside[3:]

    def sends(k):
        for r, out_ref in enumerate(outs):
            yield jnp.bitwise_xor(base, k) == r, pltpu.make_async_copy(made.at[k], out_ref, gone.at[k])

    for step, k in enumerate((0, 2, 1, 3)):
        for fetch in {0: fetches[:5], 2: fetches[5:]}.get(step, ()):
            fetch.wait()
        done = rotated_rows(*weights[k % 2 * 2 : k % 2 * 2 + 2], table_ref.at[k % 2], grads, k % 2, k // 2)
        made[k] = done
        for here, copy in sends(k):
            pl.when(here)(copy.start)
    for k in range(4):
        for here, copy in sends(k):
            pl.when(here)(copy.wait)


def rotate(base, weights, table, grads):
    rows, tokens = weights[0].shape[0] // 2, grads[0].shape[0] // 2
    given = (*grads, *weights)
    return pl.pallas_call(
        rotate_kernel,
        out_shape=[jax.ShapeDtypeStruct((rows, tokens), jnp.bfloat16)] * 4,
        in_specs=[SMEM, VMEM] + [pl.BlockSpec(memory_space=pl.ANY)] * 7,
        out_specs=[pl.BlockSpec(memory_space=pl.ANY)] * 4,
        scratch_shapes=[pltpu.VMEM(array.shape, array.dtype) for array in given]
        + [pltpu.VMEM((4, rows, tokens), jnp.bfloat16)]
        + [pltpu.SemaphoreType.DMA((7,)), pltpu.SemaphoreType.DMA((4,))],
        compiler_params=pltpu.CompilerParams(vmem_limit_bytes=40 * 1024 * 1024),
        cost_estimate=pl.CostEstimate(flops=0, bytes_accessed=0, transcendentals=0),
        name="rotate",
    )(base, table, *given)


def back_kernel(rounds, here_ref, *refs):
    pieces, (limit_ref, table_ref), (out_ref, made, gone) = refs[: len(rounds)], refs[len(rounds) :][:2], refs[-3:]
    rows = made.shape[1]
    blocks = rows // HB
    copies = []
    for i, (r, piece) in enumerate(zip(rounds, pieces)):
        quarter = jnp.bitwise_xor(here_ref[0], r)
        for b in range(blocks):
            limit = limit_ref[quarter * blocks + b]
            at = slice(b * HB, (b + 1) * HB)
            values = jnp.clip(piece[at, :].astype(jnp.float32), -limit, limit).astype(jnp.bfloat16)
            turned = jnp.dot(table_ref[quarter * blocks + b], values, preferred_element_type=jnp.float32)
            made[i, at, :] = (turned * HB**-0.5).astype(jnp.bfloat16)
        place = pl.ds(pl.multiple_of(quarter * rows, rows), rows)
        copies.append(pltpu.make_async_copy(made.at[i], out_ref.at[place, :], gone.at[i]))
        copies[-1].start()
    for copy in copies:
        copy.wait()


def back(here, pieces, rounds, limit, table, *out):
    rows, tokens = pieces[0].shape
    anywhere = pl.BlockSpec(memory_space=pl.ANY)
    operands = (here, *pieces, limit, table, *out)
    return pl.pallas_call(
        functools.partial(back_kernel, rounds),
        out_shape=jax.ShapeDtypeStruct((4 * rows, tokens), jnp.bfloat16),
        in_specs=[SMEM] + [VMEM] * (len(pieces) + 2) + [anywhere] * len(out),
        out_specs=anywhere,
        scratch_shapes=[pltpu.VMEM((len(rounds), rows, tokens), jnp.bfloat16), pltpu.SemaphoreType.DMA((len(rounds),))],
        input_output_aliases={len(operands) - 1: 0} if out else {},
        compiler_params=pltpu.CompilerParams(vmem_limit_bytes=40 * 1024 * 1024),
        cost_estimate=pl.CostEstimate(flops=0, bytes_accessed=0, transcendentals=0),
        name="rotate_back",
    )(*operands)


def product_kernel(block_ref, inputs_ref, got_ref, grads_ref, other_ref, *rest):
    arrived, (out_ref, held, done) = rest[:-3], rest[-3:]
    tile = held.shape[2]
    tiles = got_ref.shape[1] // tile
    sum_rows = (((0,), (0,)), ((), ()))
    start = block_ref[0] * tiles

    def fetch(i):
        at = pl.ds(pl.multiple_of((start + i) * tile, tile), tile)
        return pltpu.make_async_copy(inputs_ref.at[:, at], held.at[i % 2], done.at[i % 2])

    fetch(0).start()
    for i in range(tiles):
        if i + 1 < tiles:
            fetch(i + 1).start()
        fetch(i).wait()
        at = slice(i * tile, (i + 1) * tile)
        total = lax.dot_general(held[i % 2], grads_ref[...], sum_rows, preferred_element_type=jnp.float32)
        total += lax.dot_general(got_ref[:, at], other_ref[...], sum_rows, preferred_element_type=jnp.float32)
        for piece in arrived:
            total += piece[at, :].astype(jnp.float32)
        out_ref[at, :] = total.astype(out_ref.dtype)


def product(inputs, block, got, grads, other, dtype, *arrived):
    tokens, columns = grads.shape
    rows = got.shape[1]
    return pl.pallas_call(
        product_kernel,
        out_shape=jax.ShapeDtypeStruct((rows, columns), dtype),
        in_specs=[SMEM, pl.BlockSpec(memory_space=pltpu.HBM)] + [VMEM] * (3 + len(arrived)),
        out_specs=VMEM,
        scratch_shapes=[pltpu.VMEM((2, tokens, rows // 4), inputs.dtype), pltpu.SemaphoreType.DMA((2,))],
        compiler_params=pltpu.CompilerParams(vmem_limit_bytes=40 * 1024 * 1024),
        cost_estimate=pl.CostEstimate(flops=0, bytes_accessed=0, transcendentals=0),
        name="weight_product",
    )(block, inputs, got, grads, other, *arrived)


def body(earlier_inputs, earlier_grads, current_grads, key_value_weight, exponents, sign_bits):
    chip, core, tensor = (lax.axis_index(axis) for axis in AXES[1:])
    dp = chip * lax.axis_size("core") + core
    parts = lax.axis_size("tensor")
    inputs_local, grads_before, weight_local = earlier_inputs[0], earlier_grads[0], key_value_weight[0]
    rows_here = weight_local.shape[0]
    quarter = rows_here // parts

    def scalar(value):
        return jnp.reshape(value, (1,)).astype(jnp.int32)

    def features(inputs, block):
        return lax.dynamic_slice_in_dim(inputs, block * rows_here, rows_here, 1)

    def down(shard, turn=0):
        return send(shard, lambda s, d, t: (s - 1, d ^ 2, t ^ turn))

    def over_z(shard, even, odd):
        return send(shard, lambda s, d, t: (s, d, t ^ (odd if d & 1 else even)))

    def quarter_for(weight, x):
        return lax.dynamic_slice_in_dim(weight, jnp.bitwise_xor(tensor, x) * quarter, quarter, 0)

    def signed(bits, shape):
        return plain * (2 * bits - 1).astype(jnp.float32).reshape(shape)

    tokens, columns = current_grads.shape[1:]
    plain = hadamard_signs(HB)
    ahead, behind = quarter_for(weight_local, 1 + 2 * core), quarter_for(weight_local, 3 - 2 * core)
    sliced = ahead
    pair = [over_z(ahead, 1, 3), over_z(behind, 3, 1)]
    limit = (FP8_LIMIT * jnp.exp2(exponents[0].astype(jnp.float32))).astype(jnp.bfloat16)
    blocks = limit.shape[0]
    limit = jnp.pad(limit, ((0, -blocks % 16), (0, 0)))
    grads_far = down(jnp.concatenate([current_grads[0], limit], axis=0))

    inputs_then = after(inputs_local, sliced)
    grads_other = other_core(grads_before)
    got_far = other_core(features(inputs_then, jnp.bitwise_xor(dp, 3)))
    weight_then = after(weight_local, got_far)
    here, opposite = quarter_for(weight_then, 0), quarter_for(weight_then, 2)
    partial = product(
        inputs_local, scalar(jnp.bitwise_xor(dp, 2)), got_far, grads_before, grads_other, jnp.bfloat16
    )
    grads_far, partial, here, opposite, *pair = lax.optimization_barrier(
        (grads_far, partial, here, opposite, *pair)
    )

    grads_near = other_chip(grads_far)
    pair = down(jnp.concatenate(pair, axis=0))
    opposite = over_z(opposite, 2, 2)
    arrived = other_chip(after(partial, grads_near))
    bits = lax.dynamic_slice_in_dim(sign_bits, dp * quarter, quarter, 0)
    bits = send(bits, lambda s, d, t: (s, t ^ 2, d))
    rest = down(after(jnp.concatenate([here, opposite], axis=0), grads_near))
    got_near = features(after(inputs_local, grads_far), jnp.bitwise_xor(dp, 1))
    grads_near, plain, bits, got_near = lax.optimization_barrier((grads_near, plain, bits, got_near))

    limit = grads_near[tokens : tokens + blocks]
    held = jnp.concatenate([grads_near[:tokens], grads_far[:tokens]], axis=0)
    got_near = other_core(got_near)
    step_a = over_z(held, 1, 3)
    step_a, pair, bits_other = lax.optimization_barrier((step_a, pair, other_core(bits)))
    step_b = over_z(jnp.stack([held, step_a]), 3, 1)
    weights = (pair, rest, other_core(pair), other_core(rest))
    step_b, got_near, *weights = lax.optimization_barrier((step_b, got_near, *weights))

    signs_there = jnp.concatenate([bits, bits_other]).reshape(2, -1, 1, HB)
    table = signed(signs_there, signs_there.shape).astype(jnp.bfloat16)
    table = jnp.concatenate([table, table], axis=3)
    turned = rotate(scalar(jnp.bitwise_xor(dp, tensor)), weights, table, (held, step_a, step_b))
    arrived, *later = lax.optimization_barrier((arrived, *turned[2:]))
    turned = [*turned[:2], *later]

    pieces = [
        send(turned[r], lambda s, d, t, r=r: (s, (t ^ r) & 2 | d & 1, (d & 2 ^ 2) | (t ^ r) & 1)) for r in range(parts)
    ]
    limit = limit.astype(jnp.float32)[:, None, :]
    weight_grad = product(
        inputs_local, scalar(dp), got_near, grads_before, grads_other, jnp.float32, arrived
    )
    place = scalar(chip * 2 + jnp.bitwise_and(tensor, 1))
    table = signed(sign_bits, (-1, HB, 1)).astype(jnp.bfloat16)
    upstream_grad = back(place, pieces[:2], (0, 1), limit, table)
    upstream_grad = back(place, pieces[2:], (2, 3), limit, table, upstream_grad)
    return (upstream_grad[None], weight_grad[None])


def solution(mesh):
    sections, dps, tensors = (mesh.shape[axis] for axis in ("section", "dp", "tensor"))
    split = Mesh(mesh.devices.reshape(sections, dps // 2, 2, tensors), AXES)
    dp = ("chip", "core")
    placed = (
        P("section", dp, None),
        P("section", dp, "tensor"),
        P("section", dp, "tensor"),
        P("section", dp, "tensor"),
        P("section", "tensor", dp),
        P("tensor"),
    )
    return jax.shard_map(
        body,
        mesh=split,
        in_specs=placed,
        out_specs=(P("section", "tensor", dp), P("section", dp, "tensor")),
        check_vma=False,
    )
```

```python
import functools

import jax
import jax.numpy as jnp
from jax import lax
from jax.experimental import pallas as pl
from jax.experimental.pallas import tpu as pltpu
from jax.sharding import Mesh
from jax.sharding import PartitionSpec as P

HB = 128
FP8_LIMIT = 448.0
LONG = 100_000_000_000
AXES = ("section", "chip", "core", "tensor")
VMEM = pl.BlockSpec(memory_space=pltpu.VMEM)
SMEM = pl.BlockSpec(memory_space=pltpu.SMEM)


def send(shard, place):
    sections, chips, cores, tensors = (lax.axis_size(axis) for axis in AXES)
    dps = chips * cores
    pairs = []
    for s in range(sections):
        for d in range(dps):
            for t in range(tensors):
                to_s, to_d, to_t = place(s, d, t)
                if 0 <= to_s < sections:
                    pairs.append(((s * dps + d) * tensors + t, (to_s * dps + to_d) * tensors + to_t % tensors))
    return lax.ppermute(shard, AXES, pairs)


def other_core(shard):
    return send(shard, lambda s, d, t: (s, d ^ 1, t))


def other_chip(shard):
    return send(shard, lambda s, d, t: (s, d ^ 2, t))


def signs_kernel(table_ref):
    order = table_ref.shape[0]
    both = lax.broadcasted_iota(jnp.int32, (order, order), 0) & lax.broadcasted_iota(jnp.int32, (order, order), 1)
    odd = jnp.zeros_like(both)
    for bit in range(order.bit_length() - 1):
        odd = odd ^ (both >> bit & 1)
    table_ref[...] = (1 - 2 * odd).astype(jnp.float32)


def hadamard_signs(order):
    return pl.pallas_call(
        signs_kernel,
        out_shape=jax.ShapeDtypeStruct((order, order), jnp.float32),
        out_specs=VMEM,
        cost_estimate=pl.CostEstimate(flops=LONG, bytes_accessed=0, transcendentals=0),
        name="hadamard_signs",
    )()


def after(value, *others):
    return lax.optimization_barrier((value, *others))[0]


def rotated_rows(pair, rest, table_ref, grads_refs, swapped, far):
    held_ref, a_ref, b_ref = grads_refs
    rows, tokens = pair.shape[0] // 2, held_ref.shape[0] // 2
    at = slice(far * tokens, (far + 1) * tokens)
    first, second = slice(0, rows), slice(rows, 2 * rows)
    total = None
    for weight, grads in (
        (rest[first, :], held_ref[at, :]),
        (pair[second if swapped else first, :], a_ref[at, :]),
        (pair[first if swapped else second, :], b_ref[0, at, :]),
        (rest[second, :], b_ref[1, at, :]),
    ):
        term = lax.dot_general(weight, grads, (((1,), (1,)), ((), ())), preferred_element_type=jnp.float32)
        total = term if total is None else total + term
    high = total.astype(jnp.bfloat16)
    low = (total - high.astype(jnp.float32)).astype(jnp.bfloat16)
    turned = []
    for b in range(rows // HB):
        both = jnp.concatenate([high[b * HB : (b + 1) * HB], low[b * HB : (b + 1) * HB]], axis=0)
        turned.append((jnp.dot(table_ref[b], both, preferred_element_type=jnp.float32) * HB**-0.5).astype(jnp.bfloat16))
    return jnp.concatenate(turned, axis=0)


def rotate_kernel(base_ref, table_ref, *refs):
    base = base_ref[0]
    given, outs, inside, made, come, gone = refs[:7], refs[7:11], refs[11:18], refs[18], refs[19], refs[20]
    extra = given[3].shape[0] - inside[3].shape[0]
    moves = list(zip(given[:3], inside[:3]))
    for pair, rest, pair_in, rest_in in ((*given[3:5], *inside[3:5]), (*given[5:], *inside[5:])):
        held = pair_in.shape[0]
        moves += [(pair.at[:held, :], pair_in), (pair.at[held:, :], rest_in.at[:extra, :]), (rest, rest_in.at[extra:, :])]
    fetches = [pltpu.make_async_copy(far, near, come.at[i]) for i, (far, near) in enumerate(moves)]
    for fetch in fetches:
        fetch.start()
    grads, weights = inside[:3], inside[3:]

    def sends(k):
        for r, out_ref in enumerate(outs):
            yield jnp.bitwise_xor(base, k) == r, pltpu.make_async_copy(made.at[k], out_ref, gone.at[k])

    for step, k in enumerate((0, 2, 1, 3)):
        for fetch in {0: fetches[:6], 2: fetches[6:]}.get(step, ()):
            fetch.wait()
        done = rotated_rows(*weights[k % 2 * 2 : k % 2 * 2 + 2], table_ref.at[k % 2], grads, k % 2, k // 2)
        made[k] = done
        for here, copy in sends(k):
            pl.when(here)(copy.start)
    for k in range(4):
        for here, copy in sends(k):
            pl.when(here)(copy.wait)


def rotate(base, weights, table, grads):
    rows, tokens = (weights[0].shape[0] + weights[1].shape[0]) // 4, grads[0].shape[0] // 2
    given = (*grads, *weights)
    inside = [array.shape for array in grads] + [(2 * rows, weights[0].shape[1])] * 4
    return pl.pallas_call(
        rotate_kernel,
        out_shape=[jax.ShapeDtypeStruct((rows, tokens), jnp.bfloat16)] * 4,
        in_specs=[SMEM, VMEM] + [pl.BlockSpec(memory_space=pl.ANY)] * 7,
        out_specs=[pl.BlockSpec(memory_space=pl.ANY)] * 4,
        scratch_shapes=[pltpu.VMEM(shape, jnp.bfloat16) for shape in inside]
        + [pltpu.VMEM((4, rows, tokens), jnp.bfloat16)]
        + [pltpu.SemaphoreType.DMA((9,)), pltpu.SemaphoreType.DMA((4,))],
        compiler_params=pltpu.CompilerParams(vmem_limit_bytes=40 * 1024 * 1024),
        cost_estimate=pl.CostEstimate(flops=0, bytes_accessed=0, transcendentals=0),
        name="rotate",
    )(base, table, *given)


def back_kernel(rounds, here_ref, *refs):
    pieces, (limit_ref, table_ref), (out_ref, made, gone) = refs[: len(rounds)], refs[len(rounds) :][:2], refs[-3:]
    rows = made.shape[1]
    blocks = rows // HB
    copies = []
    for i, (r, piece) in enumerate(zip(rounds, pieces)):
        quarter = jnp.bitwise_xor(here_ref[0], r)
        for b in range(blocks):
            limit = limit_ref[quarter * blocks + b]
            at = slice(b * HB, (b + 1) * HB)
            values = jnp.clip(piece[at, :].astype(jnp.float32), -limit, limit).astype(jnp.bfloat16)
            turned = jnp.dot(table_ref[quarter * blocks + b], values, preferred_element_type=jnp.float32)
            made[i, at, :] = (turned * HB**-0.5).astype(jnp.bfloat16)
        place = pl.ds(pl.multiple_of(quarter * rows, rows), rows)
        copies.append(pltpu.make_async_copy(made.at[i], out_ref.at[place, :], gone.at[i]))
        copies[-1].start()
    for copy in copies:
        copy.wait()


def back(here, pieces, rounds, limit, table, *out):
    rows, tokens = pieces[0].shape
    anywhere = pl.BlockSpec(memory_space=pl.ANY)
    operands = (here, *pieces, limit, table, *out)
    return pl.pallas_call(
        functools.partial(back_kernel, rounds),
        out_shape=jax.ShapeDtypeStruct((4 * rows, tokens), jnp.bfloat16),
        in_specs=[SMEM] + [VMEM] * (len(pieces) + 2) + [anywhere] * len(out),
        out_specs=anywhere,
        scratch_shapes=[pltpu.VMEM((len(rounds), rows, tokens), jnp.bfloat16), pltpu.SemaphoreType.DMA((len(rounds),))],
        input_output_aliases={len(operands) - 1: 0} if out else {},
        compiler_params=pltpu.CompilerParams(vmem_limit_bytes=40 * 1024 * 1024),
        cost_estimate=pl.CostEstimate(flops=0, bytes_accessed=0, transcendentals=0),
        name="rotate_back",
    )(*operands)


def product_kernel(block_ref, inputs_ref, got_ref, grads_ref, other_ref, *rest):
    arrived, (out_ref, held, done) = rest[:-3], rest[-3:]
    tile = held.shape[2]
    tiles = got_ref.shape[1] // tile
    sum_rows = (((0,), (0,)), ((), ()))
    start = block_ref[0] * tiles

    def fetch(i):
        at = pl.ds(pl.multiple_of((start + i) * tile, tile), tile)
        return pltpu.make_async_copy(inputs_ref.at[:, at], held.at[i % 2], done.at[i % 2])

    fetch(0).start()
    for i in range(tiles):
        if i + 1 < tiles:
            fetch(i + 1).start()
        fetch(i).wait()
        at = slice(i * tile, (i + 1) * tile)
        total = lax.dot_general(held[i % 2], grads_ref[...], sum_rows, preferred_element_type=jnp.float32)
        total += lax.dot_general(got_ref[:, at], other_ref[...], sum_rows, preferred_element_type=jnp.float32)
        for piece in arrived:
            total += piece[at, :].astype(jnp.float32)
        out_ref[at, :] = total.astype(out_ref.dtype)


def product(inputs, block, got, grads, other, dtype, *arrived):
    tokens, columns = grads.shape
    rows = got.shape[1]
    return pl.pallas_call(
        product_kernel,
        out_shape=jax.ShapeDtypeStruct((rows, columns), dtype),
        in_specs=[SMEM, pl.BlockSpec(memory_space=pltpu.HBM)] + [VMEM] * (3 + len(arrived)),
        out_specs=VMEM,
        scratch_shapes=[pltpu.VMEM((2, tokens, rows // 4), inputs.dtype), pltpu.SemaphoreType.DMA((2,))],
        compiler_params=pltpu.CompilerParams(vmem_limit_bytes=40 * 1024 * 1024),
        cost_estimate=pl.CostEstimate(flops=0, bytes_accessed=0, transcendentals=0),
        name="weight_product",
    )(block, inputs, got, grads, other, *arrived)


def body(earlier_inputs, earlier_grads, current_grads, key_value_weight, exponents, sign_bits):
    chip, core, tensor = (lax.axis_index(axis) for axis in AXES[1:])
    dp = chip * lax.axis_size("core") + core
    parts = lax.axis_size("tensor")
    inputs_local, grads_before, weight_local = earlier_inputs[0], earlier_grads[0], key_value_weight[0]
    rows_here = weight_local.shape[0]
    quarter = rows_here // parts

    def scalar(value):
        return jnp.reshape(value, (1,)).astype(jnp.int32)

    def features(inputs, block):
        return lax.dynamic_slice_in_dim(inputs, block * rows_here, rows_here, 1)

    def down(shard, turn=0):
        return send(shard, lambda s, d, t: (s - 1, d ^ 2, t ^ turn))

    def over_z(shard, even, odd):
        return send(shard, lambda s, d, t: (s, d, t ^ (odd if d & 1 else even)))

    def quarter_for(weight, x):
        return lax.dynamic_slice_in_dim(weight, jnp.bitwise_xor(tensor, x) * quarter, quarter, 0)

    def signed(bits, shape):
        return plain * (2 * bits - 1).astype(jnp.float32).reshape(shape)

    tokens, columns = current_grads.shape[1:]
    plain = hadamard_signs(HB)
    ahead, behind = quarter_for(weight_local, 1 + 2 * core), quarter_for(weight_local, 3 - 2 * core)
    sliced = ahead
    pair = [over_z(ahead, 1, 3), over_z(behind, 3, 1)]
    limit = (FP8_LIMIT * jnp.exp2(exponents[0].astype(jnp.float32))).astype(jnp.bfloat16)
    blocks = limit.shape[0]
    limit = jnp.pad(limit, ((0, -blocks % 16), (0, 0)))
    grads_far = down(jnp.concatenate([current_grads[0], limit], axis=0))

    inputs_then = after(inputs_local, sliced)
    grads_other = other_core(grads_before)
    got_far = other_core(features(inputs_then, jnp.bitwise_xor(dp, 3)))
    weight_then = after(weight_local, got_far)
    here, opposite = quarter_for(weight_then, 0), quarter_for(weight_then, 2)
    partial = product(
        inputs_local, scalar(jnp.bitwise_xor(dp, 2)), got_far, grads_before, grads_other, jnp.bfloat16
    )
    grads_far, partial, here, opposite, *pair = lax.optimization_barrier(
        (grads_far, partial, here, opposite, *pair)
    )

    grads_near = other_chip(grads_far)
    pair = down(jnp.concatenate([*pair, here[:HB]], axis=0))
    opposite = over_z(opposite, 2, 2)
    arrived = other_chip(after(partial, grads_near))
    bits = lax.dynamic_slice_in_dim(sign_bits, dp * quarter, quarter, 0)
    bits = send(bits, lambda s, d, t: (s, t ^ 2, d))
    rest = down(after(jnp.concatenate([here[HB:], opposite], axis=0), grads_near))
    got_near = features(after(inputs_local, grads_far), jnp.bitwise_xor(dp, 1))
    grads_near, plain, bits, got_near = lax.optimization_barrier((grads_near, plain, bits, got_near))

    limit = grads_near[tokens : tokens + blocks]
    held = jnp.concatenate([grads_near[:tokens], grads_far[:tokens]], axis=0)
    got_near = other_core(got_near)
    step_a = over_z(held, 1, 3)
    step_a, pair, bits_other = lax.optimization_barrier((step_a, pair, other_core(bits)))
    step_b = over_z(jnp.stack([held, step_a]), 3, 1)
    weights = (pair, rest, other_core(pair), other_core(rest))
    step_b, got_near, *weights = lax.optimization_barrier((step_b, got_near, *weights))

    signs_there = jnp.concatenate([bits, bits_other]).reshape(2, -1, 1, HB)
    table = signed(signs_there, signs_there.shape).astype(jnp.bfloat16)
    table = jnp.concatenate([table, table], axis=3)
    turned = rotate(scalar(jnp.bitwise_xor(dp, tensor)), weights, table, (held, step_a, step_b))
    arrived, *later = lax.optimization_barrier((arrived, *turned[2:]))
    turned = [*turned[:2], *later]

    pieces = [
        send(turned[r], lambda s, d, t, r=r: (s, (t ^ r) & 2 | d & 1, (d & 2 ^ 2) | (t ^ r) & 1)) for r in range(parts)
    ]
    limit = limit.astype(jnp.float32)[:, None, :]
    weight_grad = product(
        inputs_local, scalar(dp), got_near, grads_before, grads_other, jnp.float32, arrived
    )
    place = scalar(chip * 2 + jnp.bitwise_and(tensor, 1))
    table = signed(sign_bits, (-1, HB, 1)).astype(jnp.bfloat16)
    upstream_grad = back(place, pieces[:2], (0, 1), limit, table)
    upstream_grad = back(place, pieces[2:], (2, 3), limit, table, upstream_grad)
    return (upstream_grad[None], weight_grad[None])


def solution(mesh):
    sections, dps, tensors = (mesh.shape[axis] for axis in ("section", "dp", "tensor"))
    split = Mesh(mesh.devices.reshape(sections, dps // 2, 2, tensors), AXES)
    dp = ("chip", "core")
    placed = (
        P("section", dp, None),
        P("section", dp, "tensor"),
        P("section", dp, "tensor"),
        P("section", dp, "tensor"),
        P("section", "tensor", dp),
        P("tensor"),
    )
    return jax.shard_map(
        body,
        mesh=split,
        in_specs=placed,
        out_specs=(P("section", "tensor", dp), P("section", dp, "tensor")),
        check_vma=False,
    )
```

```python
import functools

import jax
import jax.numpy as jnp
from jax import lax
from jax.experimental import pallas as pl
from jax.experimental.pallas import tpu as pltpu
from jax.sharding import Mesh
from jax.sharding import PartitionSpec as P

HB = 128
FP8_LIMIT = 448.0
LONG = 100_000_000_000
AXES = ("section", "chip", "core", "tensor")
VMEM = pl.BlockSpec(memory_space=pltpu.VMEM)
SMEM = pl.BlockSpec(memory_space=pltpu.SMEM)


def send(shard, place):
    sections, chips, cores, tensors = (lax.axis_size(axis) for axis in AXES)
    dps = chips * cores
    pairs = []
    for s in range(sections):
        for d in range(dps):
            for t in range(tensors):
                to_s, to_d, to_t = place(s, d, t)
                if 0 <= to_s < sections:
                    pairs.append(((s * dps + d) * tensors + t, (to_s * dps + to_d) * tensors + to_t % tensors))
    return lax.ppermute(shard, AXES, pairs)


def other_core(shard):
    return send(shard, lambda s, d, t: (s, d ^ 1, t))


def other_chip(shard):
    return send(shard, lambda s, d, t: (s, d ^ 2, t))


def signs_kernel(table_ref):
    order = table_ref.shape[0]
    both = lax.broadcasted_iota(jnp.int32, (order, order), 0) & lax.broadcasted_iota(jnp.int32, (order, order), 1)
    odd = jnp.zeros_like(both)
    for bit in range(order.bit_length() - 1):
        odd = odd ^ (both >> bit & 1)
    table_ref[...] = (1 - 2 * odd).astype(jnp.float32)


def hadamard_signs(order):
    return pl.pallas_call(
        signs_kernel,
        out_shape=jax.ShapeDtypeStruct((order, order), jnp.float32),
        out_specs=VMEM,
        cost_estimate=pl.CostEstimate(flops=LONG, bytes_accessed=0, transcendentals=0),
        name="hadamard_signs",
    )()


def after(value, *others):
    return lax.optimization_barrier((value, *others))[0]


def rotated_rows(pair, rest, table_ref, grads_refs, swapped, far):
    held_ref, a_ref, b_ref = grads_refs
    rows, tokens = pair.shape[0] // 2, held_ref.shape[0] // 2
    at = slice(far * tokens, (far + 1) * tokens)
    first, second = slice(0, rows), slice(rows, 2 * rows)
    total = None
    for weight, grads in (
        (rest[first, :], held_ref[at, :]),
        (pair[second if swapped else first, :], a_ref[at, :]),
        (pair[first if swapped else second, :], b_ref[0, at, :]),
        (rest[second, :], b_ref[1, at, :]),
    ):
        term = lax.dot_general(weight, grads, (((1,), (1,)), ((), ())), preferred_element_type=jnp.float32)
        total = term if total is None else total + term
    high = total.astype(jnp.bfloat16)
    low = (total - high.astype(jnp.float32)).astype(jnp.bfloat16)
    turned = []
    for b in range(rows // HB):
        both = jnp.concatenate([high[b * HB : (b + 1) * HB], low[b * HB : (b + 1) * HB]], axis=0)
        turned.append((jnp.dot(table_ref[b], both, preferred_element_type=jnp.float32) * HB**-0.5).astype(jnp.bfloat16))
    return jnp.concatenate(turned, axis=0)


def rotate_kernel(base_ref, table_ref, *refs):
    base = base_ref[0]
    given, outs, inside, made, come, gone = refs[:7], refs[7:11], refs[11:18], refs[18], refs[19], refs[20]
    extra = given[3].shape[0] - inside[3].shape[0]
    moves = list(zip(given[:3], inside[:3]))
    for pair, rest, pair_in, rest_in in ((*given[3:5], *inside[3:5]), (*given[5:], *inside[5:])):
        held = pair_in.shape[0]
        moves += [(pair.at[:held, :], pair_in), (pair.at[held:, :], rest_in.at[:extra, :]), (rest, rest_in.at[extra:, :])]
    fetches = [pltpu.make_async_copy(far, near, come.at[i]) for i, (far, near) in enumerate(moves)]
    for fetch in fetches:
        fetch.start()
    grads, weights = inside[:3], inside[3:]

    def sends(k):
        for r, out_ref in enumerate(outs):
            yield jnp.bitwise_xor(base, k) == r, pltpu.make_async_copy(made.at[k], out_ref, gone.at[k])

    for step, k in enumerate((0, 2, 1, 3)):
        for fetch in {0: fetches[:6], 2: fetches[6:]}.get(step, ()):
            fetch.wait()
        done = rotated_rows(*weights[k % 2 * 2 : k % 2 * 2 + 2], table_ref.at[k % 2], grads, k % 2, k // 2)
        made[k] = done
        for here, copy in sends(k):
            pl.when(here)(copy.start)
    for k in range(4):
        for here, copy in sends(k):
            pl.when(here)(copy.wait)


def rotate(base, weights, table, grads):
    rows, tokens = (weights[0].shape[0] + weights[1].shape[0]) // 4, grads[0].shape[0] // 2
    given = (*grads, *weights)
    inside = [array.shape for array in grads] + [(2 * rows, weights[0].shape[1])] * 4
    return pl.pallas_call(
        rotate_kernel,
        out_shape=[jax.ShapeDtypeStruct((rows, tokens), jnp.bfloat16)] * 4,
        in_specs=[SMEM, VMEM] + [pl.BlockSpec(memory_space=pl.ANY)] * 7,
        out_specs=[pl.BlockSpec(memory_space=pl.ANY)] * 4,
        scratch_shapes=[pltpu.VMEM(shape, jnp.bfloat16) for shape in inside]
        + [pltpu.VMEM((4, rows, tokens), jnp.bfloat16)]
        + [pltpu.SemaphoreType.DMA((9,)), pltpu.SemaphoreType.DMA((4,))],
        compiler_params=pltpu.CompilerParams(vmem_limit_bytes=40 * 1024 * 1024),
        cost_estimate=pl.CostEstimate(flops=0, bytes_accessed=0, transcendentals=0),
        name="rotate",
    )(base, table, *given)


def back_kernel(rounds, here_ref, *refs):
    pieces, (limit_ref, table_ref), (out_ref, made, gone) = refs[: len(rounds)], refs[len(rounds) :][:2], refs[-3:]
    rows = made.shape[1]
    blocks = rows // HB
    copies = []
    for i, (r, piece) in enumerate(zip(rounds, pieces)):
        quarter = jnp.bitwise_xor(here_ref[0], r)
        for b in range(blocks):
            limit = limit_ref[quarter * blocks + b]
            at = slice(b * HB, (b + 1) * HB)
            values = jnp.clip(piece[at, :].astype(jnp.float32), -limit, limit).astype(jnp.bfloat16)
            turned = jnp.dot(table_ref[quarter * blocks + b], values, preferred_element_type=jnp.float32)
            made[i, at, :] = (turned * HB**-0.5).astype(jnp.bfloat16)
        place = pl.ds(pl.multiple_of(quarter * rows, rows), rows)
        copies.append(pltpu.make_async_copy(made.at[i], out_ref.at[place, :], gone.at[i]))
        copies[-1].start()
    for copy in copies:
        copy.wait()


def back(here, pieces, rounds, limit, table, *out):
    rows, tokens = pieces[0].shape
    anywhere = pl.BlockSpec(memory_space=pl.ANY)
    operands = (here, *pieces, limit, table, *out)
    return pl.pallas_call(
        functools.partial(back_kernel, rounds),
        out_shape=jax.ShapeDtypeStruct((4 * rows, tokens), jnp.bfloat16),
        in_specs=[SMEM] + [VMEM] * (len(pieces) + 2) + [anywhere] * len(out),
        out_specs=anywhere,
        scratch_shapes=[pltpu.VMEM((len(rounds), rows, tokens), jnp.bfloat16), pltpu.SemaphoreType.DMA((len(rounds),))],
        input_output_aliases={len(operands) - 1: 0} if out else {},
        compiler_params=pltpu.CompilerParams(vmem_limit_bytes=40 * 1024 * 1024),
        cost_estimate=pl.CostEstimate(flops=0, bytes_accessed=0, transcendentals=0),
        name="rotate_back",
    )(*operands)


def product_kernel(block_ref, inputs_ref, got_ref, grads_ref, other_ref, *rest):
    arrived, (out_ref, held, done) = rest[:-3], rest[-3:]
    tile = held.shape[2]
    tiles = got_ref.shape[1] // tile
    sum_rows = (((0,), (0,)), ((), ()))
    start = block_ref[0] * tiles

    def fetch(i):
        at = pl.ds(pl.multiple_of((start + i) * tile, tile), tile)
        return pltpu.make_async_copy(inputs_ref.at[:, at], held.at[i % 2], done.at[i % 2])

    fetch(0).start()
    for i in range(tiles):
        if i + 1 < tiles:
            fetch(i + 1).start()
        fetch(i).wait()
        at = slice(i * tile, (i + 1) * tile)
        total = lax.dot_general(held[i % 2], grads_ref[...], sum_rows, preferred_element_type=jnp.float32)
        total += lax.dot_general(got_ref[:, at], other_ref[...], sum_rows, preferred_element_type=jnp.float32)
        for piece in arrived:
            total += piece[at, :].astype(jnp.float32)
        out_ref[at, :] = total.astype(out_ref.dtype)


def product(inputs, block, got, grads, other, dtype, *arrived):
    tokens, columns = grads.shape
    rows = got.shape[1]
    return pl.pallas_call(
        product_kernel,
        out_shape=jax.ShapeDtypeStruct((rows, columns), dtype),
        in_specs=[SMEM, pl.BlockSpec(memory_space=pltpu.HBM)] + [VMEM] * (3 + len(arrived)),
        out_specs=VMEM,
        scratch_shapes=[pltpu.VMEM((2, tokens, rows // 4), inputs.dtype), pltpu.SemaphoreType.DMA((2,))],
        compiler_params=pltpu.CompilerParams(vmem_limit_bytes=40 * 1024 * 1024),
        cost_estimate=pl.CostEstimate(flops=0, bytes_accessed=0, transcendentals=0),
        name="weight_product",
    )(block, inputs, got, grads, other, *arrived)


def body(earlier_inputs, earlier_grads, current_grads, key_value_weight, exponents, sign_bits):
    chip, core, tensor = (lax.axis_index(axis) for axis in AXES[1:])
    dp = chip * lax.axis_size("core") + core
    parts = lax.axis_size("tensor")
    inputs_local, grads_before, weight_local = earlier_inputs[0], earlier_grads[0], key_value_weight[0]
    rows_here = weight_local.shape[0]
    quarter = rows_here // parts

    def scalar(value):
        return jnp.reshape(value, (1,)).astype(jnp.int32)

    def features(inputs, block):
        return lax.dynamic_slice_in_dim(inputs, block * rows_here, rows_here, 1)

    def down(shard, turn=0):
        return send(shard, lambda s, d, t: (s - 1, d ^ 2, t ^ turn))

    def over_z(shard, even, odd):
        return send(shard, lambda s, d, t: (s, d, t ^ (odd if d & 1 else even)))

    def quarter_for(weight, x):
        return lax.dynamic_slice_in_dim(weight, jnp.bitwise_xor(tensor, x) * quarter, quarter, 0)

    def signed(bits, shape):
        return plain * (2 * bits - 1).astype(jnp.float32).reshape(shape)

    tokens, columns = current_grads.shape[1:]
    plain = hadamard_signs(HB)
    ahead, behind = quarter_for(weight_local, 1 + 2 * core), quarter_for(weight_local, 3 - 2 * core)
    sliced = ahead
    pair = [over_z(ahead, 1, 3), over_z(behind, 3, 1)]
    limit = (FP8_LIMIT * jnp.exp2(exponents[0].astype(jnp.float32))).astype(jnp.bfloat16)
    blocks = limit.shape[0]
    limit = jnp.pad(limit, ((0, -blocks % 16), (0, 0)))
    grads_far = down(jnp.concatenate([current_grads[0], limit], axis=0))

    grads_other = other_core(grads_before)
    for_far = features(after(inputs_local, sliced), jnp.bitwise_xor(dp, 3))
    weight_then = after(weight_local, sliced)
    here, opposite = quarter_for(weight_then, 0), quarter_for(weight_then, 2)
    grads_far, grads_other, for_far, here, opposite, *pair = lax.optimization_barrier(
        (grads_far, grads_other, for_far, here, opposite, *pair)
    )

    grads_near = other_chip(grads_far)
    pair = down(jnp.concatenate([*pair, here[:HB]], axis=0))
    opposite = over_z(opposite, 2, 2)
    got_far = other_core(for_far)
    partial = product(
        inputs_local, scalar(jnp.bitwise_xor(dp, 2)), got_far, grads_before, grads_other, jnp.bfloat16
    )
    grads_near, partial = lax.optimization_barrier((grads_near, partial))
    arrived = other_chip(partial)
    bits = lax.dynamic_slice_in_dim(sign_bits, dp * quarter, quarter, 0)
    bits = send(bits, lambda s, d, t: (s, t ^ 2, d))
    rest = down(after(jnp.concatenate([here[HB:], opposite], axis=0), grads_near))
    got_near = features(after(inputs_local, grads_far), jnp.bitwise_xor(dp, 1))
    grads_near, plain, bits, got_near = lax.optimization_barrier((grads_near, plain, bits, got_near))

    limit = grads_near[tokens : tokens + blocks]
    held = jnp.concatenate([grads_near[:tokens], grads_far[:tokens]], axis=0)
    got_near = other_core(got_near)
    step_a = over_z(held, 1, 3)
    step_a, pair, bits_other = lax.optimization_barrier((step_a, pair, other_core(bits)))
    step_b = over_z(jnp.stack([held, step_a]), 3, 1)
    weights = (pair, rest, other_core(pair), other_core(rest))
    step_b, got_near, *weights = lax.optimization_barrier((step_b, got_near, *weights))

    signs_there = jnp.concatenate([bits, bits_other]).reshape(2, -1, 1, HB)
    table = signed(signs_there, signs_there.shape).astype(jnp.bfloat16)
    table = jnp.concatenate([table, table], axis=3)
    turned = rotate(scalar(jnp.bitwise_xor(dp, tensor)), weights, table, (held, step_a, step_b))
    arrived, *later = lax.optimization_barrier((arrived, *turned[2:]))
    turned = [*turned[:2], *later]

    pieces = [
        send(turned[r], lambda s, d, t, r=r: (s, (t ^ r) & 2 | d & 1, (d & 2 ^ 2) | (t ^ r) & 1)) for r in range(parts)
    ]
    limit = limit.astype(jnp.float32)[:, None, :]
    weight_grad = product(
        inputs_local, scalar(dp), got_near, grads_before, grads_other, jnp.float32, arrived
    )
    place = scalar(chip * 2 + jnp.bitwise_and(tensor, 1))
    table = signed(sign_bits, (-1, HB, 1)).astype(jnp.bfloat16)
    limit, weight_grad = lax.optimization_barrier((limit, weight_grad))
    upstream_grad = back(place, pieces[:2], (0, 1), limit, table)
    upstream_grad = back(place, pieces[2:], (2, 3), limit, table, upstream_grad)
    return (upstream_grad[None], weight_grad[None])


def solution(mesh):
    sections, dps, tensors = (mesh.shape[axis] for axis in ("section", "dp", "tensor"))
    split = Mesh(mesh.devices.reshape(sections, dps // 2, 2, tensors), AXES)
    dp = ("chip", "core")
    placed = (
        P("section", dp, None),
        P("section", dp, "tensor"),
        P("section", dp, "tensor"),
        P("section", dp, "tensor"),
        P("section", "tensor", dp),
        P("tensor"),
    )
    return jax.shard_map(
        body,
        mesh=split,
        in_specs=placed,
        out_specs=(P("section", "tensor", dp), P("section", dp, "tensor")),
        check_vma=False,
    )
```

```python
import functools

import jax
import jax.numpy as jnp
from jax import lax
from jax.experimental import pallas as pl
from jax.experimental.pallas import tpu as pltpu
from jax.sharding import Mesh
from jax.sharding import PartitionSpec as P

HB = 128
FP8_LIMIT = 448.0
LONG = 100_000_000_000
AXES = ("section", "chip", "core", "tensor")
VMEM = pl.BlockSpec(memory_space=pltpu.VMEM)
SMEM = pl.BlockSpec(memory_space=pltpu.SMEM)


def send(shard, place):
    sections, chips, cores, tensors = (lax.axis_size(axis) for axis in AXES)
    dps = chips * cores
    pairs = []
    for s in range(sections):
        for d in range(dps):
            for t in range(tensors):
                to_s, to_d, to_t = place(s, d, t)
                if 0 <= to_s < sections:
                    pairs.append(((s * dps + d) * tensors + t, (to_s * dps + to_d) * tensors + to_t % tensors))
    return lax.ppermute(shard, AXES, pairs)


def other_core(shard):
    return send(shard, lambda s, d, t: (s, d ^ 1, t))


def other_chip(shard):
    return send(shard, lambda s, d, t: (s, d ^ 2, t))


def signs_kernel(table_ref):
    order = table_ref.shape[0]
    both = lax.broadcasted_iota(jnp.int32, (order, order), 0) & lax.broadcasted_iota(jnp.int32, (order, order), 1)
    odd = jnp.zeros_like(both)
    for bit in range(order.bit_length() - 1):
        odd = odd ^ (both >> bit & 1)
    table_ref[...] = (1 - 2 * odd).astype(jnp.float32)


def hadamard_signs(order):
    return pl.pallas_call(
        signs_kernel,
        out_shape=jax.ShapeDtypeStruct((order, order), jnp.float32),
        out_specs=VMEM,
        cost_estimate=pl.CostEstimate(flops=LONG, bytes_accessed=0, transcendentals=0),
        name="hadamard_signs",
    )()


def after(value, *others):
    return lax.optimization_barrier((value, *others))[0]


def rotated_rows(pair, rest, table_ref, grads_refs, swapped, far, waits):
    held_ref, a_ref, b_ref = grads_refs
    rows, tokens = pair.shape[0] // 2, held_ref.shape[0] // 2
    at = slice(far * tokens, (far + 1) * tokens)
    first, second = slice(0, rows), slice(rows, 2 * rows)
    total = None
    for wait, weight, row, (grads_ref, index) in zip(
        waits,
        (rest, pair, pair, rest),
        (first, second if swapped else first, first if swapped else second, second),
        ((held_ref, (at,)), (a_ref, (at,)), (b_ref, (0, at)), (b_ref, (1, at))),
    ):
        for fetch in wait:
            fetch.wait()
        term = lax.dot_general(
            weight[row, :], grads_ref[index], (((1,), (1,)), ((), ())), preferred_element_type=jnp.float32
        )
        total = term if total is None else total + term
    high = total.astype(jnp.bfloat16)
    low = (total - high.astype(jnp.float32)).astype(jnp.bfloat16)
    turned = []
    for b in range(rows // HB):
        both = jnp.concatenate([high[b * HB : (b + 1) * HB], low[b * HB : (b + 1) * HB]], axis=0)
        turned.append((jnp.dot(table_ref[b], both, preferred_element_type=jnp.float32) * HB**-0.5).astype(jnp.bfloat16))
    return jnp.concatenate(turned, axis=0)


def rotate_kernel(base_ref, table_ref, *refs):
    base = base_ref[0]
    given, outs, inside, made, come, gone = refs[:7], refs[7:11], refs[11:18], refs[18], refs[19], refs[20]
    extra = given[3].shape[0] - inside[3].shape[0]
    moves = []
    for pair, rest, pair_in, rest_in in ((*given[3:5], *inside[3:5]), (*given[5:], *inside[5:])):
        most = pair_in.shape[0]
        moves += [(pair.at[most:, :], rest_in.at[:extra, :]), (rest, rest_in.at[extra:, :]), (pair.at[:most, :], pair_in)]
    held, a, b = zip(given[:3], inside[:3])
    moves = [held, *moves[:2], a, moves[2], b, *moves[3:]]
    fetches = [pltpu.make_async_copy(far, near, come.at[i]) for i, (far, near) in enumerate(moves)]
    for fetch in fetches:
        fetch.start()
    grads, weights = inside[:3], inside[3:]

    def sends(k):
        for r, out_ref in enumerate(outs):
            yield jnp.bitwise_xor(base, k) == r, pltpu.make_async_copy(made.at[k], out_ref, gone.at[k])

    for step, k in enumerate((0, 2, 1, 3)):
        waits = {0: (fetches[:3], fetches[3:5], fetches[5:6], ()), 2: (fetches[6:], (), (), ())}.get(step, ((),) * 4)
        done = rotated_rows(*weights[k % 2 * 2 : k % 2 * 2 + 2], table_ref.at[k % 2], grads, k % 2, k // 2, waits)
        made[k] = done
        for here, copy in sends(k):
            pl.when(here)(copy.start)
    for k in range(4):
        for here, copy in sends(k):
            pl.when(here)(copy.wait)


def rotate(base, weights, table, grads):
    rows, tokens = (weights[0].shape[0] + weights[1].shape[0]) // 4, grads[0].shape[0] // 2
    given = (*grads, *weights)
    inside = [array.shape for array in grads] + [(2 * rows, weights[0].shape[1])] * 4
    return pl.pallas_call(
        rotate_kernel,
        out_shape=[jax.ShapeDtypeStruct((rows, tokens), jnp.bfloat16)] * 4,
        in_specs=[SMEM, VMEM] + [pl.BlockSpec(memory_space=pl.ANY)] * 7,
        out_specs=[pl.BlockSpec(memory_space=pl.ANY)] * 4,
        scratch_shapes=[pltpu.VMEM(shape, jnp.bfloat16) for shape in inside]
        + [pltpu.VMEM((4, rows, tokens), jnp.bfloat16)]
        + [pltpu.SemaphoreType.DMA((9,)), pltpu.SemaphoreType.DMA((4,))],
        compiler_params=pltpu.CompilerParams(vmem_limit_bytes=40 * 1024 * 1024),
        cost_estimate=pl.CostEstimate(flops=0, bytes_accessed=0, transcendentals=0),
        name="rotate",
    )(base, table, *given)


def back_kernel(rounds, here_ref, *refs):
    pieces, (limit_ref, table_ref), (out_ref, made, gone) = refs[: len(rounds)], refs[len(rounds) :][:2], refs[-3:]
    rows = made.shape[1]
    blocks = rows // HB
    copies = []
    for i, (r, piece) in enumerate(zip(rounds, pieces)):
        quarter = jnp.bitwise_xor(here_ref[0], r)
        for b in range(blocks):
            limit = limit_ref[quarter * blocks + b]
            at = slice(b * HB, (b + 1) * HB)
            values = jnp.clip(piece[at, :].astype(jnp.float32), -limit, limit).astype(jnp.bfloat16)
            turned = jnp.dot(table_ref[quarter * blocks + b], values, preferred_element_type=jnp.float32)
            made[i, at, :] = (turned * HB**-0.5).astype(jnp.bfloat16)
        place = pl.ds(pl.multiple_of(quarter * rows, rows), rows)
        copies.append(pltpu.make_async_copy(made.at[i], out_ref.at[place, :], gone.at[i]))
        copies[-1].start()
    for copy in copies:
        copy.wait()


def back(here, pieces, rounds, limit, table, *out):
    rows, tokens = pieces[0].shape
    anywhere = pl.BlockSpec(memory_space=pl.ANY)
    operands = (here, *pieces, limit, table, *out)
    return pl.pallas_call(
        functools.partial(back_kernel, rounds),
        out_shape=jax.ShapeDtypeStruct((4 * rows, tokens), jnp.bfloat16),
        in_specs=[SMEM] + [VMEM] * (len(pieces) + 2) + [anywhere] * len(out),
        out_specs=anywhere,
        scratch_shapes=[pltpu.VMEM((len(rounds), rows, tokens), jnp.bfloat16), pltpu.SemaphoreType.DMA((len(rounds),))],
        input_output_aliases={len(operands) - 1: 0} if out else {},
        compiler_params=pltpu.CompilerParams(vmem_limit_bytes=40 * 1024 * 1024),
        cost_estimate=pl.CostEstimate(flops=0, bytes_accessed=0, transcendentals=0),
        name="rotate_back",
    )(*operands)


def product_kernel(block_ref, inputs_ref, got_ref, grads_ref, other_ref, *rest):
    arrived, (out_ref, held, done) = rest[:-3], rest[-3:]
    tile = held.shape[2]
    tiles = got_ref.shape[1] // tile
    sum_rows = (((0,), (0,)), ((), ()))
    start = block_ref[0] * tiles

    def fetch(i):
        at = pl.ds(pl.multiple_of((start + i) * tile, tile), tile)
        return pltpu.make_async_copy(inputs_ref.at[:, at], held.at[i % 2], done.at[i % 2])

    fetch(0).start()
    for i in range(tiles):
        if i + 1 < tiles:
            fetch(i + 1).start()
        fetch(i).wait()
        at = slice(i * tile, (i + 1) * tile)
        total = lax.dot_general(held[i % 2], grads_ref[...], sum_rows, preferred_element_type=jnp.float32)
        total += lax.dot_general(got_ref[:, at], other_ref[...], sum_rows, preferred_element_type=jnp.float32)
        for piece in arrived:
            total += piece[at, :].astype(jnp.float32)
        out_ref[at, :] = total.astype(out_ref.dtype)


def product(inputs, block, got, grads, other, dtype, *arrived):
    tokens, columns = grads.shape
    rows = got.shape[1]
    return pl.pallas_call(
        product_kernel,
        out_shape=jax.ShapeDtypeStruct((rows, columns), dtype),
        in_specs=[SMEM, pl.BlockSpec(memory_space=pltpu.HBM)] + [VMEM] * (3 + len(arrived)),
        out_specs=VMEM,
        scratch_shapes=[pltpu.VMEM((2, tokens, rows // 4), inputs.dtype), pltpu.SemaphoreType.DMA((2,))],
        compiler_params=pltpu.CompilerParams(vmem_limit_bytes=40 * 1024 * 1024),
        cost_estimate=pl.CostEstimate(flops=0, bytes_accessed=0, transcendentals=0),
        name="weight_product",
    )(block, inputs, got, grads, other, *arrived)


def body(earlier_inputs, earlier_grads, current_grads, key_value_weight, exponents, sign_bits):
    chip, core, tensor = (lax.axis_index(axis) for axis in AXES[1:])
    dp = chip * lax.axis_size("core") + core
    parts = lax.axis_size("tensor")
    inputs_local, grads_before, weight_local = earlier_inputs[0], earlier_grads[0], key_value_weight[0]
    rows_here = weight_local.shape[0]
    quarter = rows_here // parts

    def scalar(value):
        return jnp.reshape(value, (1,)).astype(jnp.int32)

    def features(inputs, block):
        return lax.dynamic_slice_in_dim(inputs, block * rows_here, rows_here, 1)

    def down(shard, turn=0):
        return send(shard, lambda s, d, t: (s - 1, d ^ 2, t ^ turn))

    def over_z(shard, even, odd):
        return send(shard, lambda s, d, t: (s, d, t ^ (odd if d & 1 else even)))

    def quarter_for(weight, x):
        return lax.dynamic_slice_in_dim(weight, jnp.bitwise_xor(tensor, x) * quarter, quarter, 0)

    def signed(bits, shape):
        return plain * (2 * bits - 1).astype(jnp.float32).reshape(shape)

    tokens, columns = current_grads.shape[1:]
    plain = hadamard_signs(HB)
    ahead, behind = quarter_for(weight_local, 1 + 2 * core), quarter_for(weight_local, 3 - 2 * core)
    sliced = ahead
    pair = [over_z(ahead, 1, 3), over_z(behind, 3, 1)]
    limit = (FP8_LIMIT * jnp.exp2(exponents[0].astype(jnp.float32))).astype(jnp.bfloat16)
    blocks = limit.shape[0]
    limit = jnp.pad(limit, ((0, -blocks % 16), (0, 0)))
    grads_far = down(jnp.concatenate([current_grads[0], limit], axis=0))

    grads_other = other_core(grads_before)
    for_far = features(after(inputs_local, sliced), jnp.bitwise_xor(dp, 3))
    weight_then = after(weight_local, sliced)
    here, opposite = quarter_for(weight_then, 0), quarter_for(weight_then, 2)
    grads_far, grads_other, for_far, here, opposite, *pair = lax.optimization_barrier(
        (grads_far, grads_other, for_far, here, opposite, *pair)
    )

    grads_near = other_chip(grads_far)
    pair = down(jnp.concatenate([*pair, here[:HB]], axis=0))
    opposite = over_z(opposite, 2, 2)
    got_far = other_core(for_far)
    partial = product(
        inputs_local, scalar(jnp.bitwise_xor(dp, 2)), got_far, grads_before, grads_other, jnp.bfloat16
    )
    grads_near, partial = lax.optimization_barrier((grads_near, partial))
    arrived = other_chip(partial)
    bits = lax.dynamic_slice_in_dim(sign_bits, dp * quarter, quarter, 0)
    bits = send(bits, lambda s, d, t: (s, t ^ 2, d))
    rest = down(after(jnp.concatenate([here[HB:], opposite], axis=0), grads_near))
    got_near = features(after(inputs_local, grads_far), jnp.bitwise_xor(dp, 1))
    grads_near, plain, bits, got_near = lax.optimization_barrier((grads_near, plain, bits, got_near))

    limit = grads_near[tokens : tokens + blocks]
    held = jnp.concatenate([grads_near[:tokens], grads_far[:tokens]], axis=0)
    got_near = other_core(got_near)
    step_a = over_z(held, 1, 3)
    step_a, pair, bits_other = lax.optimization_barrier((step_a, pair, other_core(bits)))
    step_b = over_z(jnp.stack([held, step_a]), 3, 1)
    weights = (pair, rest, other_core(pair), other_core(rest))
    step_b, got_near, *weights = lax.optimization_barrier((step_b, got_near, *weights))

    signs_there = jnp.concatenate([bits, bits_other]).reshape(2, -1, 1, HB)
    table = signed(signs_there, signs_there.shape).astype(jnp.bfloat16)
    table = jnp.concatenate([table, table], axis=3)
    turned = rotate(scalar(jnp.bitwise_xor(dp, tensor)), weights, table, (held, step_a, step_b))
    arrived, *later = lax.optimization_barrier((arrived, *turned[2:]))
    turned = [*turned[:2], *later]

    pieces = [
        send(turned[r], lambda s, d, t, r=r: (s, (t ^ r) & 2 | d & 1, (d & 2 ^ 2) | (t ^ r) & 1)) for r in range(parts)
    ]
    limit = limit.astype(jnp.float32)[:, None, :]
    weight_grad = product(
        inputs_local, scalar(dp), got_near, grads_before, grads_other, jnp.float32, arrived
    )
    place = scalar(chip * 2 + jnp.bitwise_and(tensor, 1))
    table = signed(sign_bits, (-1, HB, 1)).astype(jnp.bfloat16)
    limit, weight_grad = lax.optimization_barrier((limit, weight_grad))
    upstream_grad = back(place, pieces[:2], (0, 1), limit, table)
    upstream_grad = back(place, pieces[2:], (2, 3), limit, table, upstream_grad)
    return (upstream_grad[None], weight_grad[None])


def solution(mesh):
    sections, dps, tensors = (mesh.shape[axis] for axis in ("section", "dp", "tensor"))
    split = Mesh(mesh.devices.reshape(sections, dps // 2, 2, tensors), AXES)
    dp = ("chip", "core")
    placed = (
        P("section", dp, None),
        P("section", dp, "tensor"),
        P("section", dp, "tensor"),
        P("section", dp, "tensor"),
        P("section", "tensor", dp),
        P("tensor"),
    )
    return jax.shard_map(
        body,
        mesh=split,
        in_specs=placed,
        out_specs=(P("section", "tensor", dp), P("section", dp, "tensor")),
        check_vma=False,
    )
```
